128 devices in a mesh: cell: 8 (over z_hi, y), blk: 16 (over z_lo, x, core).
Axes of the slice: x: 4, y: 4, z: 4 (z_hi: 2, z_lo: 2; z = z_hi * 2 + z_lo), core: 2. Of those that a mesh axis runs over, the one named last changes fastest.
Arguments:
- codes: bfloat16 [65536, 128], P(('cell', 'blk')), may hold values from -60 to 60
- scales: float32 [65536], P(('cell', 'blk')), may hold values from 0.5 to 2
- coarse_ids: int32 [65536], P(('cell', 'blk')), may hold values from 0 to 7, as said below
- centroids: bfloat16 [131072, 128], P(('cell', 'blk')), may hold values from -6 to 6
Outputs:
- reconstruction: bfloat16 [65536, 128], P(('cell', 'blk'))
- residual: bfloat16 [65536, 128], P(('cell', 'blk'))
The draws below stay inside these ranges and needn't reach their ends.
Inputs may be any that keep to these rules, and one draw needn't show every extreme that they name: `coarse_ids`: on every device, the number of its 512 rows that name partition g is the same for all devices; at most 128 rows of one device name one partition, and one partition is named by exactly 128 rows of every device.
All inputs are finite; a program needn't handle non-finite values.
Results may differ from the reference program's by a relative error of at most 0.006.
Values may be sent and summed in bfloat16 or wider, within the bound.
A program may use at most 256 MiB of HBM per device.

```python
import math
import jax
import jax.numpy as jnp
from jax import lax

D = 128
CENT_DEV = 1024
ROWS_DEV = 512
CENTROIDS = 131072
TOKENS = 65536
N_CELL = 8
N_BLK = 16


def loop_counts(key):
    loops = N_CELL
    cap = 2 * ROWS_DEV // loops
    rest = ROWS_DEV - cap
    base = rest // (loops - 1)
    extra = rest - base * (loops - 1)
    first, second = jax.random.split(jax.random.fold_in(key, 101))
    hot = jax.random.randint(first, (), 0, loops)
    shifts = jax.random.randint(second, (loops - 1,), 0, base // 2 + 1)
    others = base + shifts - jnp.roll(shifts, 1) + (jnp.arange(loops - 1) < extra).astype(jnp.int32)
    index = jnp.arange(loops, dtype=jnp.int32)
    picked = jnp.take(others, jnp.clip(index - (index > hot).astype(jnp.int32), 0, loops - 2))
    return jnp.where(index == hot, cap, picked).astype(jnp.int32)


def coarse_draw(key):
    bounds = jnp.cumsum(loop_counts(key))
    place = jnp.arange(ROWS_DEV, dtype=jnp.int32)
    sequence = jnp.sum((place[:, None] >= bounds[None, :]).astype(jnp.int32), axis=1)
    keys = jax.random.split(jax.random.fold_in(key, 102), N_CELL * N_BLK)

    def shuffle(one_key):
        return jax.random.permutation(one_key, ROWS_DEV)
    perms = jax.vmap(shuffle)(keys)
    return sequence[perms].reshape(TOKENS).astype(jnp.int32)


def centroid_draw(key):
    first = jax.random.fold_in(jax.random.fold_in(key, 202), 0)
    return jnp.clip(jax.random.normal(first, (CENTROIDS, D), jnp.float32), -6.0, 6.0)


def draw_coarse_ids(key, part):
    return coarse_draw(key)


def draw_centroids(key, part):
    return centroid_draw(key).astype(jnp.bfloat16)


def draw_codes(key, part):
    first = jax.random.fold_in(key, 303)
    codes = jnp.clip(jax.random.normal(first, (TOKENS, D), jnp.float32), -6.0, 6.0)
    return codes.astype(jnp.bfloat16)


def level_of(own_key, dims, cuts, least, top_value):
    gain, own = 1.0, jax.random.fold_in(own_key, 6)
    for axis_at, parts in cuts:
        heights = jnp.exp(jax.random.uniform(jax.random.fold_in(own, axis_at), (parts,), jnp.float32, least / len(cuts), top_value / len(cuts)))
        gain = gain * jnp.repeat(heights, dims[axis_at] // parts).reshape([-1 if axis == axis_at else 1 for axis in range(len(dims))])
    return gain


def setup_inputs(seed: int = 0) -> dict:
    key_of = jax.random.split(jax.random.key(seed), 5)
    codes = draw_codes(jax.random.fold_in(key_of[4], 71), 0)
    scales = jnp.clip(jnp.exp(math.log(2.0) - 1.3862944 * jax.random.uniform(key_of[1], (TOKENS,), jnp.float32) ** level_of(key_of[1], (TOKENS,), ((0, 128),), -0.2, 0.2)), 0.5, 2.0)
    coarse_ids = draw_coarse_ids(jax.random.fold_in(key_of[4], 71), 0)
    centroids = draw_centroids(jax.random.fold_in(key_of[4], 71), 0)
    return {"codes": codes, "scales": scales, "coarse_ids": coarse_ids, "centroids": centroids}


def reference(codes, scales, coarse_ids, centroids):
    width = codes.shape[1]
    beta = 1.0 / math.sqrt(width)
    loop_size = CENT_DEV * N_BLK
    dequant = (codes.astype(jnp.float32) * scales[:, None]).astype(jnp.bfloat16)
    order = jnp.argsort(coarse_ids, stable=True).astype(jnp.int32)
    sorted_rows = dequant[order]
    sorted_ids = coarse_ids[order]
    block = min(512, TOKENS)
    count_blocks = TOKENS // block
    rows_blocks = sorted_rows.reshape(count_blocks, block, width)
    ids_blocks = sorted_ids.reshape(count_blocks, block)

    def one_block(pair):
        rows, ids = pair

        def per_loop(group, carry):
            slab = lax.dynamic_slice_in_dim(centroids, (group * loop_size).astype(jnp.int32), loop_size, 0)
            scores = jnp.dot(rows, slab.T, preferred_element_type=jnp.float32) * beta
            top = lax.optimization_barrier(jnp.max(scores, axis=1))
            weights = jnp.exp(scores - top[:, None]).astype(jnp.bfloat16)
            total = lax.optimization_barrier(jnp.sum(weights.astype(jnp.float32), axis=1))
            numer = jnp.dot(weights, slab, preferred_element_type=jnp.float32)
            recon = (numer / total[:, None]).astype(jnp.bfloat16)
            return jnp.where((ids == group)[:, None], recon, carry)
        return lax.fori_loop(ids[0], ids[block - 1] + 1, per_loop, jnp.zeros((block, width), jnp.bfloat16))
    recon_sorted = lax.map(one_block, (rows_blocks, ids_blocks)).reshape(TOKENS, width)
    recon = jnp.zeros_like(recon_sorted).at[order].set(recon_sorted)
    residual = (dequant.astype(jnp.float32) - recon.astype(jnp.float32)).astype(jnp.bfloat16)
    return (recon, residual)
```

```python
import math

import jax
import jax.numpy as jnp
from jax import lax
from jax.experimental import pallas as pl
from jax.experimental.pallas import tpu as pltpu
from jax.sharding import PartitionSpec as P

D = 128
ROWS = 512
CELLS = 8
CAP = 128
SLOTS = CELLS * CAP
HALF = 512
STEP = 4 * HALF
STEPS = 8
RB = 256
NR = SLOTS // RB
SCALE = math.log2(math.e) / math.sqrt(D)
BF = jnp.bfloat16
F32 = jnp.float32
MESH = pl.DeviceIdType.MESH

(O0, O1, A0, B0, Z0, A1, B1, Z1, C0, C1, PA0, PB0, ZC0, ZC1, PA1, PB1) = range(16)


def kernel(codes_ref, scales_ref, ids_ref, cent_ref, recon_ref, resid_ref,
           buf, dequant, perm, qout, qin, qt, top, alpha, acc, ct, sbuf, pbuf, rout, rback,
           own_sem, link_send, link_recv, sib_send, sib_recv, q_send, q_recv, r_send, r_recv):
    cell, blk = lax.axis_index("cell"), lax.axis_index("blk")
    core = lax.rem(blk, 2)
    x = lax.rem(blk // 2, 4)
    z = blk // 8
    right = (cell, z * 8 + lax.rem(x + 1, 4) * 2 + core)
    left = (cell, z * 8 + lax.rem(x + 3, 4) * 2 + core)
    across = (cell, (1 - z) * 8 + x * 2 + core)
    sibling = (cell, z * 8 + x * 2 + 1 - core)

    barrier = pltpu.get_barrier_semaphore()
    for d in range(1, CELLS):
        pl.semaphore_signal(barrier, inc=1, device_id=(lax.rem(cell + d, CELLS), blk), device_id_type=MESH)
    for peer in (right, left, across, sibling):
        pl.semaphore_signal(barrier, inc=1, device_id=peer, device_id_type=MESH)

    def rows_of(unit, c):
        return buf.at[pl.ds(unit * 2 * HALF + c * HALF, HALF), :]

    def link(src, unit, to):
        return pltpu.make_async_remote_copy(
            src_ref=src, dst_ref=rows_of(unit, 0), send_sem=link_send.at[unit], recv_sem=link_recv.at[unit],
            device_id=to, device_id_type=MESH)

    def twin(unit):
        src = cent_ref.at[pl.ds(unit * HALF, HALF), :] if unit in (O0, O1) else rows_of(unit, 0)
        return pltpu.make_async_remote_copy(
            src_ref=src, dst_ref=rows_of(unit, 1), send_sem=sib_send.at[unit], recv_sem=sib_recv.at[unit],
            device_id=sibling, device_id_type=MESH)

    h0 = cent_ref.at[pl.ds(0, HALF), :]
    h1 = cent_ref.at[pl.ds(HALF, HALF), :]
    links = {
        A0: (h0, right), B0: (h0, left), Z0: (h0, across),
        A1: (h1, right), B1: (h1, left), Z1: (h1, across),
        C0: (rows_of(A0, 0), right), C1: (rows_of(B1, 0), left),
        PA0: (rows_of(Z0, 0), right), PB0: (rows_of(Z0, 0), left),
        PA1: (rows_of(Z1, 0), right), PB1: (rows_of(Z1, 0), left),
        ZC0: (rows_of(C0, 0), across), ZC1: (rows_of(C1, 0), across),
    }

    def send(*units):
        for unit in units:
            link(links[unit][0], unit, links[unit][1]).start()

    def arrived(*units):
        for unit in units:
            link(links[unit][0], unit, links[unit][1]).wait_recv()
            twin(unit).start()

    def doubled(*units):
        for unit in units:
            twin(unit).wait_recv()

    own = [pltpu.make_async_copy(cent_ref.at[pl.ds(h * HALF, HALF), :], rows_of(h, 0), own_sem.at[h]) for h in (0, 1)]
    for copy in own:
        copy.start()

    ids = ids_ref[...]
    scales = scales_ref[...]
    for a in range(ROWS // 128):
        rs = slice(a * 128, (a + 1) * 128)
        column = jnp.broadcast_to(scales[:, rs], (128, 128)).T
        dequant[rs, :] = (codes_ref[rs, :].astype(F32) * column).astype(BF)
    onehot = lax.broadcasted_iota(jnp.int32, (CELLS, ROWS), 0) == ids
    before = lax.broadcasted_iota(jnp.int32, (ROWS, ROWS), 0) <= lax.broadcasted_iota(jnp.int32, (ROWS, ROWS), 1)
    counts = jnp.dot(onehot.astype(F32).astype(BF), before.astype(F32).astype(BF), preferred_element_type=F32)
    rank = jnp.sum(jnp.where(onehot, counts, 0.0), axis=0, keepdims=True) - 1.0
    slot = ids * CAP + rank.astype(jnp.int32)
    spread = (lax.broadcasted_iota(jnp.int32, (SLOTS, ROWS), 0) == slot).astype(F32).astype(BF)
    qout[...] = jnp.dot(spread, dequant[...], preferred_element_type=F32).astype(BF)

    pl.semaphore_wait(barrier, CELLS - 1 + 4)
    twin(O0).start()
    twin(O1).start()

    def block(ref, at):
        return ref.at[pl.ds(pl.multiple_of(at * CAP, CAP), CAP), :]

    def queries(d):
        to = lax.rem(cell + d, CELLS)
        return pltpu.make_async_remote_copy(
            src_ref=block(qout, to), dst_ref=block(qin, cell), send_sem=q_send.at[d], recv_sem=q_recv.at[d],
            device_id=(to, blk), device_id_type=MESH)

    def results(d):
        to = lax.rem(cell + d, CELLS)
        return pltpu.make_async_remote_copy(
            src_ref=block(rout, to), dst_ref=block(rback, cell), send_sem=r_send.at[d], recv_sem=r_recv.at[d],
            device_id=(to, blk), device_id_type=MESH)

    for d in range(1, CELLS):
        queries(d).start()
    send(A0, B0, Z0, A1, B1, Z1)
    mine = pl.ds(pl.multiple_of(cell * CAP, CAP), CAP)
    qin[mine, :] = qout[mine, :]

    places = jnp.broadcast_to(slot, (128, ROWS)).T
    for g in range(CELLS):
        hit = places == g * CAP + lax.broadcasted_iota(jnp.int32, (ROWS, CAP), 1)
        perm[:, g * CAP:(g + 1) * CAP] = hit.astype(F32).astype(BF)
    top[...] = jnp.full_like(top, -1e30)
    alpha[...] = jnp.ones_like(alpha)
    acc[...] = jnp.zeros_like(acc)
    sbuf[...] = jnp.full_like(sbuf, -1e30)
    pbuf[...] = jnp.zeros_like(pbuf)
    ct[...] = jnp.zeros_like(ct)
    for d in range(1, CELLS):
        queries(d).wait_recv()
    qt[...] = qin[...].T

    def stage_scores(c, r):
        rs = slice(r * RB, (r + 1) * RB)
        s = jnp.dot(c, qt[:, rs], preferred_element_type=F32) * SCALE
        old = top[:, rs]
        new = jnp.maximum(old, jnp.max(s, axis=0, keepdims=True))
        sbuf[r % 2] = s
        alpha[:, rs] = jnp.exp2(old - new)
        top[:, rs] = new

    def stage_weights(r):
        rs = slice(r * RB, (r + 1) * RB)
        pbuf[r % 2] = jnp.exp2(sbuf[r % 2] - top[0:1, rs]).astype(BF)

    def stage_sums(r, at):
        rs = slice(r * RB, (r + 1) * RB)
        acc[:, rs] = acc[:, rs] * alpha[0:1, rs] + jnp.dot(ct[at], pbuf[r % 2], preferred_element_type=F32)

    def step(i, at):
        c = buf[pl.ds(pl.multiple_of(i * STEP, STEP), STEP), :]
        ct[at, 0:D, :] = c.T
        ct[at, D:, :] = jnp.ones((16, STEP), BF)
        for r in range(NR):
            stage_scores(c, r)
            stage_weights((r - 1) % NR)
            stage_sums((r - 2) % NR, at if r >= 2 else 1 - at)

    def pair(j, _):
        @pl.when(j == 0)
        def _():
            for copy in own:
                copy.wait()
            doubled(O0, O1)

        @pl.when(j == 1)
        def _():
            arrived(A1, B1, Z1)
            send(C1, PA1, PB1)
            doubled(Z0, A1)

        @pl.when(j == 2)
        def _():
            arrived(C1)
            send(ZC1)
            doubled(C0, C1)

        @pl.when(j == 3)
        def _():
            arrived(ZC0, ZC1)
            doubled(ZC0, ZC1)
        step(2 * j, 0)

        @pl.when(j == 0)
        def _():
            arrived(A0, B0, Z0)
            send(C0, PA0, PB0)
            doubled(A0, B0)

        @pl.when(j == 1)
        def _():
            arrived(C0)
            send(ZC0)
            doubled(B1, Z1)

        @pl.when(j == 2)
        def _():
            arrived(PA0, PB0)
            doubled(PA0, PB0)

        @pl.when(j == 3)
        def _():
            arrived(PA1, PB1)
            doubled(PA1, PB1)
        step(2 * j + 1, 1)
        return 0

    lax.fori_loop(0, STEPS // 2, pair, 0)
    stage_weights(NR - 1)
    stage_sums(NR - 2, 1)
    stage_sums(NR - 1, 1)

    rout[...] = (acc[0:D, :] / acc[D:D + 1, :]).T.astype(BF)
    for d in range(1, CELLS):
        results(d).start()
    rback[mine, :] = rout[mine, :]
    for unit in links:
        link(links[unit][0], unit, links[unit][1]).wait_send()
    for unit in range(16):
        twin(unit).wait_send()
    for d in range(1, CELLS):
        queries(d).wait_send()
    for d in range(1, CELLS):
        results(d).wait_recv()
    recon = jnp.dot(perm[...], rback[...], preferred_element_type=F32)
    recon_ref[...] = recon.astype(BF)
    resid_ref[...] = (dequant[...].astype(F32) - recon).astype(BF)
    for d in range(1, CELLS):
        results(d).wait_send()


def local(codes, scales, coarse_ids, centroids):
    vmem = pl.BlockSpec(memory_space=pltpu.VMEM)
    out = jax.ShapeDtypeStruct((ROWS, D), BF)
    dma = pltpu.SemaphoreType.DMA
    return pl.pallas_call(
        kernel,
        out_shape=(out, out),
        in_specs=[vmem, vmem, vmem, pl.BlockSpec(memory_space=pl.ANY)],
        out_specs=(vmem, vmem),
        scratch_shapes=[
            pltpu.VMEM((STEPS * STEP, D), BF),
            pltpu.VMEM((ROWS, D), BF),
            pltpu.VMEM((ROWS, SLOTS), BF),
            pltpu.VMEM((SLOTS, D), BF),
            pltpu.VMEM((SLOTS, D), BF),
            pltpu.VMEM((D, SLOTS), BF),
            pltpu.VMEM((8, SLOTS), F32),
            pltpu.VMEM((8, SLOTS), F32),
            pltpu.VMEM((D + 16, SLOTS), F32),
            pltpu.VMEM((2, D + 16, STEP), BF),
            pltpu.VMEM((2, STEP, RB), F32),
            pltpu.VMEM((2, STEP, RB), BF),
            pltpu.VMEM((SLOTS, D), BF),
            pltpu.VMEM((SLOTS, D), BF),
            dma((2,)), dma((16,)), dma((16,)), dma((16,)), dma((16,)),
            dma((CELLS,)), dma((CELLS,)), dma((CELLS,)), dma((CELLS,)),
        ],
        compiler_params=pltpu.CompilerParams(
            collective_id=0, has_side_effects=True, vmem_limit_bytes=48 * 2**20),
        cost_estimate=pl.CostEstimate(
            flops=4 * SLOTS * STEPS * STEP * D, bytes_accessed=2**20, transcendentals=SLOTS * STEPS * STEP),
        name="reassign",
    )(codes, scales.reshape(1, ROWS), coarse_ids.reshape(1, ROWS), centroids)


def solution(mesh):
    both = P(("cell", "blk"), None)
    flat = P(("cell", "blk"))
    return jax.shard_map(local, mesh=mesh, in_specs=(both, flat, flat, both), out_specs=(both, both), check_vma=False)
```

```python
import math

import jax
import jax.numpy as jnp
from jax import lax
from jax.experimental import pallas as pl
from jax.experimental.pallas import tpu as pltpu
from jax.sharding import PartitionSpec as P

D = 128
ROWS = 512
CELLS = 8
CAP = 128
SLOTS = CELLS * CAP
HALF = 512
STEP = 4 * HALF
STEPS = 8
RB = 256
NR = SLOTS // RB
SCALE = math.log2(math.e) / math.sqrt(D)
BF = jnp.bfloat16
F32 = jnp.float32
MESH = pl.DeviceIdType.MESH

(O0, O1, A0, B0, Z0, A1, B1, Z1, C0, C1, PA0, PB0, ZC0, ZC1, PA1, PB1) = range(16)


NEAR = ((0, 0), (0, 1), (0, 3), (0, 2), (1, 0), (1, 1), (1, 3), (1, 2))
BACK = (0, 2, 1, 3, 4, 6, 5, 7)


def kernel(codes_hbm, scales_hbm, ids_hbm, cent_ref, recon_ref, resid_ref,
           buf, codes_ref, scales_ref, ids_ref, dequant, perm, qout, qin, qt, top, alpha, acc, ct, sbuf, rout, rback,
           own_sem, in_sem, link_send, link_recv, sib_send, sib_recv, q_send, q_recv, r_send, r_recv):
    cell, blk = lax.axis_index("cell"), lax.axis_index("blk")
    core = lax.rem(blk, 2)
    x = lax.rem(blk // 2, 4)
    z = blk // 8
    right = (cell, z * 8 + lax.rem(x + 1, 4) * 2 + core)
    left = (cell, z * 8 + lax.rem(x + 3, 4) * 2 + core)
    across = (cell, (1 - z) * 8 + x * 2 + core)
    sibling = (cell, z * 8 + x * 2 + 1 - core)

    def cell_at(dz, dy):
        return lax.rem(cell // 4 + dz, 2) * 4 + lax.rem(lax.rem(cell, 4) + dy, 4)

    barrier = pltpu.get_barrier_semaphore()
    for j in range(1, CELLS):
        pl.semaphore_signal(barrier, inc=1, device_id=(cell_at(*NEAR[j]), blk), device_id_type=MESH)
    for peer in (right, left, across, sibling):
        pl.semaphore_signal(barrier, inc=1, device_id=peer, device_id_type=MESH)

    def rows_of(unit, c):
        return buf.at[pl.ds(unit * 2 * HALF + c * HALF, HALF), :]

    def link(src, unit, to):
        return pltpu.make_async_remote_copy(
            src_ref=src, dst_ref=rows_of(unit, 0), send_sem=link_send.at[unit], recv_sem=link_recv.at[unit],
            device_id=to, device_id_type=MESH)

    def twin(unit):
        src = cent_ref.at[pl.ds(unit * HALF, HALF), :] if unit in (O0, O1) else rows_of(unit, 0)
        return pltpu.make_async_remote_copy(
            src_ref=src, dst_ref=rows_of(unit, 1), send_sem=sib_send.at[unit], recv_sem=sib_recv.at[unit],
            device_id=sibling, device_id_type=MESH)

    h0 = cent_ref.at[pl.ds(0, HALF), :]
    h1 = cent_ref.at[pl.ds(HALF, HALF), :]
    links = {
        A0: (h0, right), B0: (h0, left), Z0: (h0, across),
        A1: (h1, right), B1: (h1, left), Z1: (h1, across),
        C0: (rows_of(A0, 0), right), C1: (rows_of(B1, 0), left),
        PA0: (rows_of(Z0, 0), right), PB0: (rows_of(Z0, 0), left),
        PA1: (rows_of(Z1, 0), right), PB1: (rows_of(Z1, 0), left),
        ZC0: (rows_of(C0, 0), across), ZC1: (rows_of(C1, 0), across),
    }

    def send(*units):
        for unit in units:
            link(links[unit][0], unit, links[unit][1]).start()

    def arrived(*units):
        for unit in units:
            link(links[unit][0], unit, links[unit][1]).wait_recv()
            twin(unit).start()

    def doubled(*units):
        for unit in units:
            twin(unit).wait_recv()

    ins = [pltpu.make_async_copy(src, dst, in_sem.at[n]) for n, (src, dst) in enumerate(
        ((ids_hbm, ids_ref), (scales_hbm, scales_ref), (codes_hbm, codes_ref)))]
    own = [pltpu.make_async_copy(cent_ref.at[pl.ds(h * HALF, HALF), :], rows_of(h, 0), own_sem.at[h]) for h in (0, 1)]
    for copy in ins + own:
        copy.start()
    for copy in ins:
        copy.wait()

    ids = ids_ref[...]
    scales = scales_ref[...]
    for a in range(ROWS // 128):
        rs = slice(a * 128, (a + 1) * 128)
        column = jnp.broadcast_to(scales[:, rs], (128, 128)).T
        dequant[rs, :] = (codes_ref[rs, :].astype(F32) * column).astype(BF)
    onehot = lax.broadcasted_iota(jnp.int32, (CELLS, ROWS), 0) == ids
    before = lax.broadcasted_iota(jnp.int32, (ROWS, ROWS), 0) <= lax.broadcasted_iota(jnp.int32, (ROWS, ROWS), 1)
    counts = jnp.dot(onehot.astype(F32).astype(BF), before.astype(F32).astype(BF), preferred_element_type=F32)
    rank = jnp.sum(jnp.where(onehot, counts, 0.0), axis=0, keepdims=True) - 1.0
    slot = ids * CAP + rank.astype(jnp.int32)
    spread = (lax.broadcasted_iota(jnp.int32, (SLOTS, ROWS), 0) == slot).astype(F32).astype(BF)
    qout[...] = jnp.dot(spread, dequant[...], preferred_element_type=F32).astype(BF)

    def block(ref, at):
        return ref.at[pl.ds(pl.multiple_of(at * CAP, CAP), CAP), :]

    def queries(j):
        to = cell_at(*NEAR[j])
        return pltpu.make_async_remote_copy(
            src_ref=block(qout, to), dst_ref=block(qin, BACK[j]), send_sem=q_send.at[j], recv_sem=q_recv.at[BACK[j]],
            device_id=(to, blk), device_id_type=MESH)

    def queries_here(j):
        return pltpu.make_async_remote_copy(
            src_ref=block(qout, j), dst_ref=block(qin, j), send_sem=q_send.at[j], recv_sem=q_recv.at[j],
            device_id=(cell_at(*NEAR[j]), blk), device_id_type=MESH)

    def results(j, dz, dy, back):
        return pltpu.make_async_remote_copy(
            src_ref=block(rout, j), dst_ref=block(rback, cell), send_sem=r_send.at[j], recv_sem=r_recv.at[back],
            device_id=(cell_at(dz, dy), blk), device_id_type=MESH)

    def results_here(j):
        return pltpu.make_async_remote_copy(
            src_ref=block(rout, j), dst_ref=block(rback, cell_at(*NEAR[j])), send_sem=r_send.at[j],
            recv_sem=r_recv.at[j], device_id=(cell_at(*NEAR[j]), blk), device_id_type=MESH)

    pl.semaphore_wait(barrier, CELLS - 1 + 4)
    for j in range(CELLS - 1, 0, -1):
        queries(j).start()
    send(A0, B0, Z0, A1, B1, Z1)
    twin(O0).start()
    twin(O1).start()
    mine = pl.ds(pl.multiple_of(cell * CAP, CAP), CAP)
    qin[0:CAP, :] = qout[mine, :]

    places = jnp.broadcast_to(slot, (128, ROWS)).T
    for g in range(CELLS):
        hit = places == g * CAP + lax.broadcasted_iota(jnp.int32, (ROWS, CAP), 1)
        perm[:, g * CAP:(g + 1) * CAP] = hit.astype(F32).astype(BF)
    top[...] = jnp.full_like(top, -1e30)
    alpha[...] = jnp.ones_like(alpha)
    acc[...] = jnp.zeros_like(acc)
    sbuf[1] = jnp.full((STEP, RB), -1e30, F32)
    ct[...] = jnp.zeros_like(ct)
    for j in range(1, CELLS):
        queries_here(j).wait_recv()
    for r in range(NR):
        scaled = qin[r * RB:(r + 1) * RB, :].astype(F32) * SCALE
        high = scaled.astype(BF)
        qt[r, 0:D, :] = high.T
        qt[r, D:, :] = (scaled - high.astype(F32)).astype(BF).T

    def unit(i, r, at, n, r_was, at_was):
        q = qt[r]
        high = None
        total = None
        for k in range(2):
            ks = slice(k * (STEP // 2), (k + 1) * (STEP // 2))
            c = buf[pl.ds(pl.multiple_of(i * STEP + k * (STEP // 2), STEP // 2), STEP // 2), :]
            s = jnp.dot(jnp.concatenate([c, c], axis=1), q, preferred_element_type=F32)
            sbuf[n % 2, ks, :] = s
            peak = jnp.max(s.reshape(STEP // 16, 8, RB), axis=0)
            high = peak if high is None else jnp.maximum(high, peak)
            w = jnp.exp2(sbuf[(n + 1) % 2, ks, :] - top[r_was, 0:1, :]).astype(BF)
            part = jnp.dot(ct[at_was, :, ks], w, preferred_element_type=F32)
            total = part if total is None else total + part
        acc[r_was] = acc[r_was] * alpha[r_was, 0:1, :] + total
        old = top[r]
        new = jnp.maximum(old, jnp.max(high, axis=0, keepdims=True))
        alpha[r] = jnp.exp2(old - new)
        top[r] = new

    def turn(i, at):
        c = buf[pl.ds(pl.multiple_of(i * STEP, STEP), STEP), :]
        ct[at, 0:D, :] = c.T
        ct[at, D:, :] = jnp.ones((16, STEP), BF)

    def step(i, at):
        turn(i, at)
        for r in range(NR):
            unit(i, r, at, r, (r - 1) % NR, at if r >= 1 else 1 - at)

    def pair(j, _):
        @pl.when(j == 0)
        def _():
            for copy in own:
                copy.wait()
            doubled(O0, O1)

        @pl.when(j == 1)
        def _():
            arrived(A1, B1, Z1)
            send(C1, PA1, PB1)
            doubled(Z0, A1)

        @pl.when(j == 2)
        def _():
            arrived(C1)
            send(ZC1)
            doubled(C0, C1)
        step(2 * j, 0)

        @pl.when(j == 0)
        def _():
            arrived(A0, B0, Z0)
            send(C0, PA0, PB0)
            doubled(A0, B0)

        @pl.when(j == 1)
        def _():
            arrived(C0)
            send(ZC0)
            doubled(B1, Z1)

        @pl.when(j == 2)
        def _():
            arrived(PA0, PB0)
            doubled(PA0, PB0)
        step(2 * j + 1, 1)
        return 0

    lax.fori_loop(0, STEPS // 2 - 1, pair, 0)
    arrived(ZC0, ZC1, PA1, PB1)
    doubled(ZC0, ZC1, PA1, PB1)

    def finish(r):
        rout[pl.ds(pl.multiple_of(r * RB, RB), RB), :] = (acc[r, 0:D, :] / acc[r, D:D + 1, :]).T.astype(BF)

    def last(j, _):
        r = NR - 1 - j
        r_was = jnp.minimum(r + 1, NR - 1)
        turn(STEPS - 2, 0)
        unit(STEPS - 2, r, 0, 0, r_was, 1)
        turn(STEPS - 1, 1)
        unit(STEPS - 1, r, 1, 1, r, 0)
        finish(r_was)

        @pl.when(j > 0)
        def _():
            odd = lax.rem(r_was, 2)
            results(2 * r_was, r_was // 2, 3 * odd, 2 * r_was - odd).start()
            results(2 * r_was + 1, r_was // 2, 1 + odd, 2 * r_was + 2 - odd).start()
        return 0

    lax.fori_loop(0, NR, last, 0)
    w = jnp.exp2(sbuf[1] - top[0, 0:1, :]).astype(BF)
    acc[0] = acc[0] * alpha[0, 0:1, :] + jnp.dot(ct[1], w, preferred_element_type=F32)
    finish(0)
    results(1, 0, 1, BACK[1]).start()
    rback[mine, :] = rout[0:CAP, :]
    for unit_ in links:
        link(links[unit_][0], unit_, links[unit_][1]).wait_send()
    for unit_ in range(16):
        twin(unit_).wait_send()
    for j in range(1, CELLS):
        queries(j).wait_send()
    for j in range(1, CELLS):
        results_here(j).wait_recv()
    recon = jnp.dot(perm[...], rback[...], preferred_element_type=F32)
    recon_ref[...] = recon.astype(BF)
    resid_ref[...] = (dequant[...].astype(F32) - recon).astype(BF)
    for j in range(1, CELLS):
        results_here(j).wait_send()


def local(codes, scales, coarse_ids, centroids):
    vmem = pl.BlockSpec(memory_space=pltpu.VMEM)
    out = jax.ShapeDtypeStruct((ROWS, D), BF)
    dma = pltpu.SemaphoreType.DMA
    return pl.pallas_call(
        kernel,
        out_shape=(out, out),
        in_specs=[pl.BlockSpec(memory_space=pltpu.HBM)] * 4,
        out_specs=(vmem, vmem),
        scratch_shapes=[
            pltpu.VMEM((STEPS * STEP, D), BF),
            pltpu.VMEM((ROWS, D), BF),
            pltpu.VMEM((1, ROWS), F32),
            pltpu.VMEM((1, ROWS), jnp.int32),
            pltpu.VMEM((ROWS, D), BF),
            pltpu.VMEM((ROWS, SLOTS), BF),
            pltpu.VMEM((SLOTS, D), BF),
            pltpu.VMEM((SLOTS, D), BF),
            pltpu.VMEM((NR, 2 * D, RB), BF),
            pltpu.VMEM((NR, 8, RB), F32),
            pltpu.VMEM((NR, 8, RB), F32),
            pltpu.VMEM((NR, D + 16, RB), F32),
            pltpu.VMEM((2, D + 16, STEP), BF),
            pltpu.VMEM((2, STEP, RB), F32),
            pltpu.VMEM((SLOTS, D), BF),
            pltpu.VMEM((SLOTS, D), BF),
            dma((2,)), dma((3,)), dma((16,)), dma((16,)), dma((16,)), dma((16,)),
            dma((CELLS,)), dma((CELLS,)), dma((CELLS,)), dma((CELLS,)),
        ],
        compiler_params=pltpu.CompilerParams(
            collective_id=0, has_side_effects=True, vmem_limit_bytes=60 * 2**20),
        cost_estimate=pl.CostEstimate(
            flops=4 * SLOTS * STEPS * STEP * D, bytes_accessed=2**20, transcendentals=SLOTS * STEPS * STEP),
        name="reassign",
    )(codes, scales.reshape(1, ROWS), coarse_ids.reshape(1, ROWS), centroids)


def solution(mesh):
    both = P(("cell", "blk"), None)
    flat = P(("cell", "blk"))
    return jax.shard_map(local, mesh=mesh, in_specs=(both, flat, flat, both), out_specs=(both, both), check_vma=False)
```

```python
import math

import jax
import jax.numpy as jnp
from jax import lax
from jax.experimental import pallas as pl
from jax.experimental.pallas import tpu as pltpu
from jax.sharding import PartitionSpec as P

D = 128
ROWS = 512
CELLS = 8
CAP = 128
SLOTS = CELLS * CAP
HALF = 512
STEP = 4 * HALF
STEPS = 8
RB = 256
NR = SLOTS // RB
SCALE = math.log2(math.e) / math.sqrt(D)
BF = jnp.bfloat16
F32 = jnp.float32
MESH = pl.DeviceIdType.MESH

(O0, O1, A0, B0, Z0, A1, B1, Z1, C0, C1, PA0, PB0, ZC0, ZC1, PA1, PB1) = range(16)


ORDER = (
    (O0, 0), (O1, 0), (O0, 1), (O1, 1),
    (A0, 0), (B0, 0), (Z0, 0), (A0, 1),
    (B0, 1), (Z0, 1), (A1, 0), (B1, 0),
    (A1, 1), (B1, 1), (Z1, 0), (C0, 0),
    (Z1, 1), (C0, 1), (C1, 0), (PA0, 0),
    (C1, 1), (PA0, 1), (PB0, 0), (PA1, 0),
    (PB0, 1), (PA1, 1), (PB1, 0), (ZC0, 0),
    (PB1, 1), (ZC0, 1), (ZC1, 0), (ZC1, 1),
)

NEAR = ((0, 0), (0, 1), (0, 3), (0, 2), (1, 0), (1, 1), (1, 3), (1, 2))
BACK = (0, 2, 1, 3, 4, 6, 5, 7)


def kernel(codes_hbm, scales_hbm, ids_hbm, cent_ref, recon_ref, resid_ref,
           buf, codes_ref, scales_ref, ids_ref, dequant, perm, qout, qin, qt, top, alpha, acc, ct, sbuf, rout, rback,
           own_sem, in_sem, link_send, link_recv, sib_send, sib_recv, q_send, q_recv, r_send, r_recv):
    cell, blk = lax.axis_index("cell"), lax.axis_index("blk")
    core = lax.rem(blk, 2)
    x = lax.rem(blk // 2, 4)
    z = blk // 8
    right = (cell, z * 8 + lax.rem(x + 1, 4) * 2 + core)
    left = (cell, z * 8 + lax.rem(x + 3, 4) * 2 + core)
    across = (cell, (1 - z) * 8 + x * 2 + core)
    sibling = (cell, z * 8 + x * 2 + 1 - core)

    def cell_at(dz, dy):
        return lax.rem(cell // 4 + dz, 2) * 4 + lax.rem(lax.rem(cell, 4) + dy, 4)

    barrier = pltpu.get_barrier_semaphore()
    for j in range(1, CELLS):
        pl.semaphore_signal(barrier, inc=1, device_id=(cell_at(*NEAR[j]), blk), device_id_type=MESH)
    for peer in (right, left, across, sibling):
        pl.semaphore_signal(barrier, inc=1, device_id=peer, device_id_type=MESH)

    def rows_of(unit, c):
        return buf.at[pl.ds(ORDER.index((unit, c)) * HALF, HALF), :]

    def link(src, unit, to):
        return pltpu.make_async_remote_copy(
            src_ref=src, dst_ref=rows_of(unit, 0), send_sem=link_send.at[unit], recv_sem=link_recv.at[unit],
            device_id=to, device_id_type=MESH)

    def twin(unit):
        src = cent_ref.at[pl.ds(unit * HALF, HALF), :] if unit in (O0, O1) else rows_of(unit, 0)
        return pltpu.make_async_remote_copy(
            src_ref=src, dst_ref=rows_of(unit, 1), send_sem=sib_send.at[unit], recv_sem=sib_recv.at[unit],
            device_id=sibling, device_id_type=MESH)

    h0 = cent_ref.at[pl.ds(0, HALF), :]
    h1 = cent_ref.at[pl.ds(HALF, HALF), :]
    links = {
        A0: (h0, right), B0: (h1, left), Z0: (h0, across),
        A1: (h1, right), B1: (h0, left), Z1: (h1, across),
        C0: (rows_of(A0, 0), right), C1: (rows_of(B0, 0), left),
        PA0: (rows_of(Z0, 0), right), PB0: (rows_of(Z0, 0), left),
        PA1: (rows_of(A1, 0), across), PB1: (rows_of(Z1, 0), left),
        ZC0: (rows_of(C0, 0), across), ZC1: (rows_of(C1, 0), across),
    }

    def send(*units):
        for unit in units:
            link(links[unit][0], unit, links[unit][1]).start()

    def arrived(*units):
        for unit in units:
            link(links[unit][0], unit, links[unit][1]).wait_recv()
            twin(unit).start()

    def doubled(*units):
        for unit in units:
            twin(unit).wait_recv()

    ins = [pltpu.make_async_copy(src, dst, in_sem.at[n]) for n, (src, dst) in enumerate(
        ((ids_hbm, ids_ref), (scales_hbm, scales_ref), (codes_hbm, codes_ref)))]
    own = [pltpu.make_async_copy(cent_ref.at[pl.ds(h * HALF, HALF), :], rows_of(h, 0), own_sem.at[h]) for h in (0, 1)]
    for copy in ins + own:
        copy.start()
    for copy in ins:
        copy.wait()

    ids = ids_ref[...]
    scales = scales_ref[...]
    for a in range(ROWS // 128):
        rs = slice(a * 128, (a + 1) * 128)
        column = jnp.broadcast_to(scales[:, rs], (128, 128)).T
        dequant[rs, :] = (codes_ref[rs, :].astype(F32) * column).astype(BF)
    onehot = lax.broadcasted_iota(jnp.int32, (CELLS, ROWS), 0) == ids
    before = lax.broadcasted_iota(jnp.int32, (ROWS, ROWS), 0) <= lax.broadcasted_iota(jnp.int32, (ROWS, ROWS), 1)
    counts = jnp.dot(onehot.astype(F32).astype(BF), before.astype(F32).astype(BF), preferred_element_type=F32)
    rank = jnp.sum(jnp.where(onehot, counts, 0.0), axis=0, keepdims=True) - 1.0
    slot = ids * CAP + rank.astype(jnp.int32)
    spread = (lax.broadcasted_iota(jnp.int32, (SLOTS, ROWS), 0) == slot).astype(F32).astype(BF)
    qout[...] = jnp.dot(spread, dequant[...], preferred_element_type=F32).astype(BF)

    def block(ref, at):
        return ref.at[pl.ds(pl.multiple_of(at * CAP, CAP), CAP), :]

    def queries(j):
        to = cell_at(*NEAR[j])
        return pltpu.make_async_remote_copy(
            src_ref=block(qout, to), dst_ref=block(qin, BACK[j]), send_sem=q_send.at[j], recv_sem=q_recv.at[BACK[j]],
            device_id=(to, blk), device_id_type=MESH)

    def queries_here(j):
        return pltpu.make_async_remote_copy(
            src_ref=block(qout, j), dst_ref=block(qin, j), send_sem=q_send.at[j], recv_sem=q_recv.at[j],
            device_id=(cell_at(*NEAR[j]), blk), device_id_type=MESH)

    def results(j, dz, dy, back):
        return pltpu.make_async_remote_copy(
            src_ref=block(rout, j), dst_ref=block(rback, cell), send_sem=r_send.at[j], recv_sem=r_recv.at[back],
            device_id=(cell_at(dz, dy), blk), device_id_type=MESH)

    def results_here(j):
        return pltpu.make_async_remote_copy(
            src_ref=block(rout, j), dst_ref=block(rback, cell_at(*NEAR[j])), send_sem=r_send.at[j],
            recv_sem=r_recv.at[j], device_id=(cell_at(*NEAR[j]), blk), device_id_type=MESH)

    pl.semaphore_wait(barrier, CELLS - 1 + 4)
    for j in range(CELLS - 1, 0, -1):
        queries(j).start()
    send(A0, B0, Z0, A1, B1, Z1)
    twin(O0).start()
    twin(O1).start()
    mine = pl.ds(pl.multiple_of(cell * CAP, CAP), CAP)
    qin[0:CAP, :] = qout[mine, :]

    places = jnp.broadcast_to(slot, (128, ROWS)).T
    for g in range(CELLS):
        hit = places == g * CAP + lax.broadcasted_iota(jnp.int32, (ROWS, CAP), 1)
        perm[:, g * CAP:(g + 1) * CAP] = hit.astype(F32).astype(BF)
    top[...] = jnp.full_like(top, -1e30)
    alpha[...] = jnp.ones_like(alpha)
    acc[...] = jnp.zeros_like(acc)
    sbuf[1] = jnp.full((STEP, RB), -1e30, F32)
    ct[...] = jnp.zeros_like(ct)
    for j in range(1, CELLS):
        queries_here(j).wait_recv()
    for r in range(NR):
        scaled = qin[r * RB:(r + 1) * RB, :].astype(F32) * SCALE
        high = scaled.astype(BF)
        qt[r, 0:D, :] = high.T
        qt[r, D:, :] = (scaled - high.astype(F32)).astype(BF).T

    def unit(i, r, at, n, r_was, at_was):
        q = qt[r]
        high = None
        total = None
        for k in range(2):
            ks = slice(k * (STEP // 2), (k + 1) * (STEP // 2))
            c = buf[pl.ds(pl.multiple_of(i * STEP + k * (STEP // 2), STEP // 2), STEP // 2), :]
            s = jnp.dot(jnp.concatenate([c, c], axis=1), q, preferred_element_type=F32)
            sbuf[n % 2, ks, :] = s
            peak = jnp.max(s.reshape(STEP // 16, 8, RB), axis=0)
            high = peak if high is None else jnp.maximum(high, peak)
            w = jnp.exp2(sbuf[(n + 1) % 2, ks, :] - top[r_was, 0:1, :]).astype(BF)
            part = jnp.dot(ct[at_was, :, ks], w, preferred_element_type=F32)
            total = part if total is None else total + part
        acc[r_was] = acc[r_was] * alpha[r_was, 0:1, :] + total
        old = top[r]
        new = jnp.maximum(old, jnp.max(high, axis=0, keepdims=True))
        alpha[r] = jnp.exp2(old - new)
        top[r] = new

    def turn(i, at):
        c = buf[pl.ds(pl.multiple_of(i * STEP, STEP), STEP), :]
        ct[at, 0:D, :] = c.T
        ct[at, D:, :] = jnp.ones((16, STEP), BF)

    def step(i, at):
        turn(i, at)
        for r in range(NR):
            unit(i, r, at, r, (r - 1) % NR, at if r >= 1 else 1 - at)

    def pair(j, _):
        @pl.when(j == 0)
        def _():
            for copy in own:
                copy.wait()
            doubled(O0, O1)

        @pl.when(j == 1)
        def _():
            arrived(A1, B1)
            send(PA1)
            doubled(B0, Z0)

        @pl.when(j == 2)
        def _():
            arrived(C1, PA0)
            send(ZC1)
            doubled(Z1, C0)
        step(2 * j, 0)

        @pl.when(j == 0)
        def _():
            arrived(A0, B0, Z0)
            send(C0, C1, PA0, PB0)
            doubled(A0)

        @pl.when(j == 1)
        def _():
            arrived(Z1, C0)
            send(ZC0, PB1)
            doubled(A1, B1)

        @pl.when(j == 2)
        def _():
            arrived(PB0, PA1)
            doubled(C1, PA0)
        step(2 * j + 1, 1)
        return 0

    lax.fori_loop(0, STEPS // 2 - 1, pair, 0)
    arrived(PB1, ZC0, ZC1)
    doubled(PB0, PA1, PB1, ZC0, ZC1)

    def finish(r):
        rout[pl.ds(pl.multiple_of(r * RB, RB), RB), :] = (acc[r, 0:D, :] / acc[r, D:D + 1, :]).T.astype(BF)

    def last(j, _):
        r = NR - 1 - j
        r_was = jnp.minimum(r + 1, NR - 1)
        turn(STEPS - 2, 0)
        unit(STEPS - 2, r, 0, 0, r_was, 1)
        turn(STEPS - 1, 1)
        unit(STEPS - 1, r, 1, 1, r, 0)
        finish(r_was)

        @pl.when(j > 0)
        def _():
            odd = lax.rem(r_was, 2)
            results(2 * r_was, r_was // 2, 3 * odd, 2 * r_was - odd).start()
            results(2 * r_was + 1, r_was // 2, 1 + odd, 2 * r_was + 2 - odd).start()
        return 0

    lax.fori_loop(0, NR, last, 0)
    w = jnp.exp2(sbuf[1] - top[0, 0:1, :]).astype(BF)
    acc[0] = acc[0] * alpha[0, 0:1, :] + jnp.dot(ct[1], w, preferred_element_type=F32)
    finish(0)
    results(1, 0, 1, BACK[1]).start()
    rback[mine, :] = rout[0:CAP, :]
    for unit_ in links:
        link(links[unit_][0], unit_, links[unit_][1]).wait_send()
    for unit_ in range(16):
        twin(unit_).wait_send()
    for j in range(1, CELLS):
        queries(j).wait_send()
    for j in range(1, CELLS):
        results_here(j).wait_recv()
    recon = jnp.dot(perm[...], rback[...], preferred_element_type=F32)
    recon_ref[...] = recon.astype(BF)
    resid_ref[...] = (dequant[...].astype(F32) - recon).astype(BF)
    for j in range(1, CELLS):
        results_here(j).wait_send()


def local(codes, scales, coarse_ids, centroids):
    vmem = pl.BlockSpec(memory_space=pltpu.VMEM)
    out = jax.ShapeDtypeStruct((ROWS, D), BF)
    dma = pltpu.SemaphoreType.DMA
    return pl.pallas_call(
        kernel,
        out_shape=(out, out),
        in_specs=[pl.BlockSpec(memory_space=pltpu.HBM)] * 4,
        out_specs=(vmem, vmem),
        scratch_shapes=[
            pltpu.VMEM((STEPS * STEP, D), BF),
            pltpu.VMEM((ROWS, D), BF),
            pltpu.VMEM((1, ROWS), F32),
            pltpu.VMEM((1, ROWS), jnp.int32),
            pltpu.VMEM((ROWS, D), BF),
            pltpu.VMEM((ROWS, SLOTS), BF),
            pltpu.VMEM((SLOTS, D), BF),
            pltpu.VMEM((SLOTS, D), BF),
            pltpu.VMEM((NR, 2 * D, RB), BF),
            pltpu.VMEM((NR, 8, RB), F32),
            pltpu.VMEM((NR, 8, RB), F32),
            pltpu.VMEM((NR, D + 16, RB), F32),
            pltpu.VMEM((2, D + 16, STEP), BF),
            pltpu.VMEM((2, STEP, RB), F32),
            pltpu.VMEM((SLOTS, D), BF),
            pltpu.VMEM((SLOTS, D), BF),
            dma((2,)), dma((3,)), dma((16,)), dma((16,)), dma((16,)), dma((16,)),
            dma((CELLS,)), dma((CELLS,)), dma((CELLS,)), dma((CELLS,)),
        ],
        compiler_params=pltpu.CompilerParams(
            collective_id=0, has_side_effects=True, vmem_limit_bytes=60 * 2**20),
        cost_estimate=pl.CostEstimate(
            flops=4 * SLOTS * STEPS * STEP * D, bytes_accessed=2**20, transcendentals=SLOTS * STEPS * STEP),
        name="reassign",
    )(codes, scales.reshape(1, ROWS), coarse_ids.reshape(1, ROWS), centroids)


def solution(mesh):
    both = P(("cell", "blk"), None)
    flat = P(("cell", "blk"))
    return jax.shard_map(local, mesh=mesh, in_specs=(both, flat, flat, both), out_specs=(both, both), check_vma=False)
```
